256 devices in a mesh: row: 16 (over y, x_hi, core), col: 16 (over x_lo, z).
Axes of the slice: x: 4 (x_hi: 2, x_lo: 2; x = x_hi * 2 + x_lo), y: 4, z: 8, core: 2. Of those that a mesh axis runs over, the one named last changes fastest.
Arguments:
- features: bfloat16 [131072, 128], P(('row', 'col')), may hold values from -6 to 6
- node_order: int32 [16, 16, 512], P('row', 'col'), may hold values from 0 to 511, each once within a row
- weight: bfloat16 [128, 128], replicated, may hold values from -0.5 to 0.5
- bias: float32 [128], replicated, may hold values from -3 to 3
- tile_values: bfloat16 [16, 16, 352, 128, 128], P('row', 'col'), may hold values from -0.078125 to 0.078125
- tile_rows: int32 [16, 16, 352], P('row', 'col'), may hold values from 0 to 63, as said below
- tile_cols: int32 [16, 16, 352], P('row', 'col'), may hold values from 0 to 63, as said below
- tile_count: int32 [16, 16], P('row', 'col'), may hold values from 1 to 352, as said below
- cotangent: bfloat16 [131072, 128], P(('row', 'col')), may hold values from -6 to 6
Outputs:
- activated: bfloat16 [131072, 128], P(('row', 'col'))
- input_grad: bfloat16 [131072, 128], P(('row', 'col'))
- weight_grad: float32 [128, 128], replicated
- bias_grad: float32 [128], replicated
The draws below stay inside these ranges and needn't reach their ends.
Inputs may be any that keep to these rules, and one draw needn't show every extreme that they name: `tile_rows`: within one device the slots hold distinct (row tile, column tile) pairs, in increasing order of row tile * 64 + column tile. `tile_cols`: paired with tile_rows slot by slot. `tile_count`: the busiest device of every draw uses all 352 slots.
All inputs are finite; a program needn't handle non-finite values.
Results may differ from the reference program's by a relative error of at most 0.023.
Values may be sent and summed in bfloat16 or wider, within the bound.
No kernel may reach another device: no remote copies, remote signals or barrier semaphores. Data moves between devices by JAX's collectives and lax.ppermute only.
A program may use at most 192 MiB of HBM per device.

```python
import jax
import jax.numpy as jnp
from jax import lax

F = 128
TILE = 128
TD = 4
TMAX = 352
MESH_R = 16
MESH_C = 16
NS = 512
RB = 64
CB = 64
NODES = 131072


def tile_layout(key):
    devices = MESH_R * MESH_C
    device_keys = jax.random.split(jax.random.fold_in(key, 11), devices)

    def choose_spots(sub_key):
        chosen = jax.random.permutation(sub_key, RB * CB)[:TMAX]
        return jnp.sort(chosen)
    positions = jax.vmap(choose_spots)(device_keys).reshape(MESH_R, MESH_C, TMAX)
    return (positions // CB, positions % CB)


def draw_tile_rows(key, part):
    rows_drawn, cols_drawn = tile_layout(key)
    return rows_drawn.astype(jnp.int32)


def draw_tile_cols(key, part):
    rows_drawn, cols_drawn = tile_layout(key)
    return cols_drawn.astype(jnp.int32)


def draw_tile_count(key, part):
    key = jax.random.fold_in(key, 3)
    devices = MESH_R * MESH_C
    first_key, second_key = jax.random.split(key)
    levels = jax.random.randint(first_key, (devices,), 1, 17)
    levels = levels * levels
    busiest = jax.random.randint(second_key, (), 0, devices)
    levels = jnp.where(jnp.arange(devices) == busiest, 256, levels)
    counts = jnp.maximum(TMAX * levels // 256, 1)
    return counts.reshape(MESH_R, MESH_C).astype(jnp.int32)


def steps_of(own_key, extent, pieces, smallest, largest):
    def one(dim, shards_of):
        draws = jax.random.uniform(jax.random.fold_in(jax.random.fold_in(own_key, 6), dim), (shards_of,), jnp.float32, smallest / len(pieces), largest / len(pieces))
        return jnp.repeat(jnp.exp(draws), extent[dim] // shards_of).reshape((-1,) + (1,) * (len(extent) - dim - 1))

    gain = one(*pieces[0])
    for cut in pieces[1:]:
        gain = gain * one(*cut)
    return gain


def normal_values(rng, shape, width, reach, cuts=(), dtype=jnp.bfloat16):
    array = jax.random.normal(rng, shape, jnp.float32) * width
    if len(cuts) > 0:
        array = steps_of(rng, shape, cuts, -0.22, 0.18) * array
    return jnp.clip(array, min=-reach, max=reach).astype(dtype)


def setup_inputs(seed: int = 0) -> dict:
    splits = jax.random.split(jax.random.key(seed), 10)
    return {
        "features": normal_values(splits[0], (NODES, F), 1.0, 6.0, ((0, 256),)),
        "node_order": jax.vmap(lambda own: jax.random.permutation(own, NS))(jax.random.split(splits[1], MESH_R * MESH_C)).reshape((MESH_R, MESH_C, NS)).astype(jnp.int32),
        "weight": normal_values(splits[2], (F, F), F ** -0.5, 0.5),
        "bias": normal_values(splits[3], (F,), 0.5, 3.0, (), jnp.float32),
        "tile_values": normal_values(splits[4], (MESH_R, MESH_C, TMAX, TILE, TILE), (TILE * TMAX // (2 * TD)) ** -0.5, 0.078125, ((0, 16), (1, 16))),
        "tile_rows": draw_tile_rows(jax.random.fold_in(splits[9], 71), 0),
        "tile_cols": draw_tile_cols(jax.random.fold_in(splits[9], 71), 0),
        "tile_count": draw_tile_count(jax.random.fold_in(splits[9], 71), 0),
        "cotangent": normal_values(splits[8], (NODES, F), 1.0, 6.0, ((0, 256),)),
    }


def tile_sum(tiles, pick_index, target_index, blocks, valid, segments, transpose):
    picked = blocks[pick_index].astype(jnp.float32)
    form = 'tji,tjf->tif' if transpose else 'tij,tjf->tif'
    products = jnp.einsum(form, tiles.astype(jnp.float32), picked)
    products = products * valid[:, None, None]
    return jax.ops.segment_sum(products, target_index, num_segments=segments)


def round_term(term):
    return lax.optimization_barrier(term.astype(jnp.bfloat16)).astype(jnp.float32)


def select_rows(values, node_order):
    return jax.vmap(lambda block, perm: block[perm])(values, node_order)


def restore_rows(values, node_order):
    return jax.vmap(lambda block, perm: jnp.zeros_like(block).at[perm].set(block))(values, node_order)


def reference(features, node_order, weight, bias, tile_values, tile_rows, tile_cols, tile_count, cotangent):
    devices = MESH_R * MESH_C
    order_flat = node_order.reshape(devices, NS)
    ordered = select_rows(features.reshape(devices, NS, F), order_flat)
    projected = jnp.dot(ordered.reshape(-1, F), weight, preferred_element_type=jnp.float32).astype(jnp.bfloat16)
    projected = projected.reshape(MESH_R, MESH_C, NS, F)
    valid = (jnp.arange(TMAX)[None, None, :] < tile_count[:, :, None]).astype(jnp.float32)

    def row_slab(row_index):
        def accumulate(running, col_index):
            blocks = projected[:, col_index].reshape(CB, TILE, F)
            term = tile_sum(tile_values[row_index, col_index], tile_cols[row_index, col_index],
                            tile_rows[row_index, col_index], blocks, valid[row_index, col_index], RB, False)
            return running + round_term(term), None
        running, _ = lax.scan(accumulate, jnp.zeros((RB, TILE, F), jnp.float32), jnp.arange(MESH_C))
        return running.reshape(MESH_C, NS, F)

    aggregate = lax.map(row_slab, jnp.arange(MESH_R))
    pre_act = aggregate + bias
    sigmoid_pre = jax.nn.sigmoid(pre_act)
    activated = (pre_act * sigmoid_pre).astype(jnp.bfloat16)
    cot_ordered = select_rows(cotangent.reshape(devices, NS, F), order_flat).reshape(MESH_R, MESH_C, NS, F)
    grad_pre = cot_ordered.astype(jnp.float32) * (sigmoid_pre * (1.0 + pre_act * (1.0 - sigmoid_pre)))
    hidden_grad = grad_pre.astype(jnp.bfloat16)

    def col_slab(col_index):
        def accumulate(running, row_index):
            blocks = hidden_grad[row_index].reshape(RB, TILE, F)
            term = tile_sum(tile_values[row_index, col_index], tile_rows[row_index, col_index],
                            tile_cols[row_index, col_index], blocks, valid[row_index, col_index], CB, True)
            return running + round_term(term), None
        running, _ = lax.scan(accumulate, jnp.zeros((CB, TILE, F), jnp.float32), jnp.arange(MESH_R))
        return running.reshape(MESH_R, NS, F)

    proj_grad = jnp.transpose(lax.map(col_slab, jnp.arange(MESH_C)), (1, 0, 2, 3)).astype(jnp.bfloat16)
    proj_flat = proj_grad.reshape(-1, F)
    input_ord = jnp.dot(proj_flat, weight.T, preferred_element_type=jnp.float32).astype(jnp.bfloat16)
    weight_grad = jnp.dot(ordered.reshape(-1, F).T, proj_flat, preferred_element_type=jnp.float32)
    bias_grad = jnp.sum(grad_pre, axis=(0, 1, 2))
    activated = restore_rows(activated.reshape(devices, NS, F), order_flat).reshape(NODES, F)
    input_grad = restore_rows(input_ord.reshape(devices, NS, F), order_flat).reshape(NODES, F)
    return activated, input_grad, weight_grad, bias_grad
```

```python
import functools

import jax
import jax.numpy as jnp
import numpy as np
from jax import lax
from jax.experimental import pallas as pl
from jax.experimental.pallas import tpu as pltpu
from jax.sharding import Mesh
from jax.sharding import PartitionSpec as P

TILE = 128
CHUNK = 32
GROUP = 8
F32 = jnp.float32
BF16 = jnp.bfloat16
SIZES = {"y": 4, "xh": 2, "core": 2, "xl": 2, "z": 8}
ROW = ("y", "xh", "core")
COL = ("xl", "z")
ALL = ROW + COL
YX = ((2, 1), (1, 1), (3, 1), (2, 0), (0, 1), (1, 0), (3, 0), (0, 0))
Z = (4, 3, 5, 2, 6, 1, 7, 0)


def shifted(x, axes, delta):
    sizes = [SIZES[a] for a in axes]
    perm = []
    for i in range(int(np.prod(sizes))):
        at = np.unravel_index(i, sizes)
        to = [(a + d) % s for a, d, s in zip(at, delta, sizes)]
        perm.append((i, int(np.ravel_multi_index(to, sizes))))
    return lax.ppermute(x, axes, perm)


def one_hot_t(order_ref, nodes):
    here = lax.broadcasted_iota(jnp.int32, (nodes, nodes), 0)
    return (here == order_ref[...]).astype(BF16)


def dot(a, b, dims=((1,), (0,))):
    return lax.dot_general(a, b, (dims, ((), ())), preferred_element_type=F32)


def order_kernel(order_ref, x_ref, out_ref):
    pt = one_hot_t(order_ref, x_ref.shape[0])
    out_ref[...] = dot(pt, x_ref[...], ((0,), (0,))).astype(BF16)


def tiles_kernel(transpose, n_in, n_out, *refs):
    count_ref, rows_ref, cols_ref, in_at, out_at = refs[:5]
    tiles_ref = refs[5]
    blocks = refs[6 : 6 + n_in]
    outs = refs[6 + n_in : 6 + n_in + n_out]
    tiles, held, total, tile_sem, block_sem = refs[6 + n_in + n_out :]
    slots = tiles_ref.shape[0]
    per = blocks[0].shape[0]
    segments = held.shape[0]
    chunks = slots // CHUNK
    block_copies = [
        pltpu.make_async_copy(b, held.at[pl.ds(in_at[i] * per, per)], block_sem.at[i])
        for i, b in enumerate(blocks)
    ]
    for c in block_copies:
        c.start()
    copies = [
        pltpu.make_async_copy(
            tiles_ref.at[pl.ds(c * CHUNK, CHUNK)], tiles.at[pl.ds(c * CHUNK, CHUNK)], tile_sem.at[c]
        )
        for c in range(chunks)
    ]
    for c in copies:
        c.start()
    count = count_ref[0]

    def zero(i, _):
        total[i] = jnp.zeros((TILE, TILE), F32)
        return 0

    lax.fori_loop(0, segments, zero, 0, unroll=4)
    for c in block_copies:
        c.wait()

    def step(g, _):
        products = []
        for u in range(GROUP):
            t = g * GROUP + u
            if transpose:
                products.append((cols_ref[t], dot(held[rows_ref[t]], tiles[t])))
            else:
                products.append((rows_ref[t], dot(tiles[t], held[cols_ref[t]])))
        for u, (target, product) in enumerate(products):
            target = jnp.where(g * GROUP + u < count, target, segments)
            total[target] += product
        return 0

    for c in range(chunks):
        copies[c].wait()
        first = c * (CHUNK // GROUP)
        last = jnp.clip((count + GROUP - 1) // GROUP, first, first + CHUNK // GROUP)
        lax.fori_loop(first, last, step, 0)
    at = 0
    for out in outs:
        for k in range(out.shape[0] // per):
            out[pl.ds(k * per, per)] = total[pl.ds(out_at[at] * per, per)].astype(BF16)
            at += 1


def tile_sum(tiles, rows, cols, count, in_at, out_at, blocks, out_counts, transpose):
    slots = tiles.shape[0]
    per = blocks[0].shape[0]
    segments = len(blocks) * per
    n_in, n_out = len(blocks), len(out_counts)
    smem = pl.BlockSpec(memory_space=pltpu.SMEM)
    anywhere = pl.BlockSpec(memory_space=pl.ANY)
    return pl.pallas_call(
        functools.partial(tiles_kernel, transpose, n_in, n_out),
        out_shape=[jax.ShapeDtypeStruct((n * per, TILE, TILE), BF16) for n in out_counts],
        in_specs=[smem] * 5 + [anywhere] * (1 + n_in),
        out_specs=[pl.BlockSpec(memory_space=pltpu.VMEM)] * n_out,
        scratch_shapes=[
            pltpu.VMEM((slots, TILE, TILE), BF16),
            pltpu.VMEM((segments, TILE, TILE), BF16),
            pltpu.VMEM((segments + 1, TILE, TILE), F32),
            pltpu.SemaphoreType.DMA((slots // CHUNK,)),
            pltpu.SemaphoreType.DMA((n_in,)),
        ],
        compiler_params=pltpu.CompilerParams(vmem_limit_bytes=40 << 20),
        cost_estimate=pl.CostEstimate(
            flops=2 * slots * TILE**3, bytes_accessed=slots * TILE * TILE * 2, transcendentals=0
        ),
        name="tile_sum_t" if transpose else "tile_sum",
    )(count, rows, cols, in_at, out_at, tiles, *blocks)


def act_kernel(*refs):
    order_ref, cot_ref, weight_ref, bias_ref = refs[:4]
    parts = refs[4:12]
    gt_ref, hi_ref, lo_ref, act_ref, bias_out = refs[12:]
    nodes = cot_ref.shape[0]
    cot = dot(one_hot_t(order_ref, nodes), cot_ref[...], ((0,), (0,)))
    total = parts[0][...].astype(F32)
    for p in parts[1:]:
        total = total + p[...].astype(F32)
    hi = total.astype(BF16)
    lo = (total - hi.astype(F32)).astype(BF16)
    hi_ref[...] = hi
    lo_ref[...] = lo
    weight = weight_ref[...]
    pre = dot(hi, weight) + dot(lo, weight) + bias_ref[...]
    sig = jax.nn.sigmoid(pre)
    grad = cot * (sig * (1.0 + pre * (1.0 - sig)))
    act_ref[...] = (pre * sig).astype(BF16)
    bias_out[...] = jnp.sum(grad, axis=0, keepdims=True)
    for t in range(nodes // TILE):
        gt_ref[t] = grad[t * TILE : (t + 1) * TILE].T.astype(BF16)


def side_kernel(order_ref, act_ref, gt_ref, hi_ref, lo_ref, out_ref, weight_out):
    nodes = act_ref.shape[0]
    out_ref[...] = dot(one_hot_t(order_ref, nodes), act_ref[...]).astype(BF16)
    total = jnp.zeros((TILE, TILE), F32)
    for t in range(nodes // TILE):
        sl = pl.ds(t * TILE, TILE)
        total += dot(gt_ref[t], hi_ref[sl]) + dot(gt_ref[t], lo_ref[sl])
    weight_out[...] = total.T


def input_kernel(*refs):
    order_ref, weight_ref = refs[:2]
    parts = refs[2:10]
    out_ref = refs[10]
    nodes = out_ref.shape[0]
    total = parts[0][...].astype(F32)
    for p in parts[1:]:
        total = total + p[...].astype(F32)
    grad = total.astype(BF16)
    back = jnp.concatenate(
        [dot(weight_ref[...], grad[t]).astype(BF16) for t in range(nodes // TILE)], axis=1
    )
    out_ref[...] = dot(one_hot_t(order_ref, nodes), back, ((1,), (1,))).astype(BF16)


def add_kernel(a_ref, b_ref, *outs):
    at = 0
    for out in outs:
        n = out.shape[0]
        sl = pl.ds(at, n)
        out[...] = (a_ref[sl].astype(F32) + b_ref[sl].astype(F32)).astype(BF16)
        at += n


def call(kernel, out_shape, name, *args):
    vmem = pl.BlockSpec(memory_space=pltpu.VMEM)
    return pl.pallas_call(
        kernel,
        out_shape=out_shape,
        in_specs=[vmem] * len(args),
        out_specs=jax.tree.map(lambda _: vmem, out_shape),
        compiler_params=pltpu.CompilerParams(vmem_limit_bytes=32 << 20),
        name=name,
    )(*args)


def shape(*dims, dtype=BF16):
    return jax.ShapeDtypeStruct(dims, dtype)


def on_device(
    features, node_order, weight, bias, tile_values, tile_rows, tile_cols, tile_count, cotangent
):
    nodes, width = features.shape
    per = nodes // TILE
    order = node_order.reshape(1, nodes)
    tiles = tile_values[0, 0]
    rows, cols, count = tile_rows[0, 0], tile_cols[0, 0], tile_count[0]
    me = {a: lax.axis_index(a) for a in ALL}

    def place(axes, delta, sign):
        at = 0
        for a, d in zip(axes, delta):
            at = at * SIZES[a] + lax.rem(me[a] + sign * d + SIZES[a], SIZES[a])
        return at

    row_shifts = [yx + (c,) for c in (0, 1) for yx in YX]
    col_shifts = [(x, z) for x in (0, 1) for z in Z]
    x_at = jnp.stack([place(ROW, d, -1) for d in row_shifts]).astype(jnp.int32)
    g_at = jnp.stack([place(COL, d, -1) for d in col_shifts]).astype(jnp.int32)
    agg_at = jnp.stack([place(COL, d, 1) for d in col_shifts]).astype(jnp.int32)
    grad_at = jnp.stack([place(ROW, d, 1) for d in row_shifts]).astype(jnp.int32)

    block = shape(per, TILE, TILE)
    ordered = call(order_kernel, shape(nodes, width), "order", order, features)
    ordered = ordered.reshape(per, TILE, width)
    xs = [shifted(ordered, ("y", "xh"), d) for d in YX[:-1]] + [ordered]
    xs = xs + [shifted(x, ("core",), (1,)) for x in xs]

    pieces = tile_sum(tiles, rows, cols, count, x_at, agg_at, xs, (2,) * 8, False)
    mine, theirs = pieces[:4], pieces[4:]
    got = [shifted(t, ("xl",), (1,)) for t in theirs]
    agg = []
    for i in range(4):
        two = call(add_kernel, [block, block], "add_two", mine[i], got[i])
        for j in range(2):
            z = Z[2 * i + j]
            agg.append(shifted(two[j], ("z",), (z,)) if z else two[j])
    agg = [a.reshape(nodes, width) for a in agg]

    gt, hi, lo, act, bias_part = call(
        act_kernel,
        [block, shape(nodes, width), shape(nodes, width), shape(nodes, width), shape(1, width, dtype=F32)],
        "act",
        order,
        cotangent,
        weight,
        bias.reshape(1, width),
        *agg,
    )
    gs = [shifted(gt, ("z",), (z,)) for z in Z[:-1]] + [gt]
    gs = gs + [shifted(g, ("xl",), (1,)) for g in gs]
    activated, weight_part = call(
        side_kernel,
        [shape(nodes, width), shape(width, width, dtype=F32)],
        "side",
        order,
        act,
        gt,
        hi,
        lo,
    )
    devices = int(np.prod([SIZES[a] for a in ALL]))
    flat = jnp.concatenate([weight_part, bias_part], axis=0).reshape(-1)
    share = -(-flat.shape[0] // devices)
    share = -(-share // TILE) * TILE
    flat = jnp.pad(flat, (0, devices * share - flat.shape[0])).reshape(devices, share)
    summed = jnp.sum(lax.all_to_all(flat, ALL, 0, 0, tiled=True), axis=0, keepdims=True)
    summed = lax.all_to_all(jnp.broadcast_to(summed, (devices, share)), ALL, 0, 0, tiled=True)
    summed = summed.reshape(-1)
    weight_grad = summed[: width * width].reshape(width, width)
    bias_grad = summed[width * width : width * width + width]

    mine, theirs = tile_sum(tiles, rows, cols, count, g_at, grad_at, gs, (8, 8), True)
    got = shifted(theirs, ("core",), (1,))
    parts = call(add_kernel, [block] * 8, "add_eight", mine, got)
    parts = [shifted(p, ("y", "xh"), d) for p, d in zip(parts[:-1], YX[:-1])] + [parts[-1]]
    input_grad = call(input_kernel, shape(nodes, width), "input", order, weight, *parts)
    return activated, input_grad, weight_grad, bias_grad


def solution(mesh):
    fine = Mesh(mesh.devices.reshape([SIZES[a] for a in ALL]), ALL)
    in_specs = (
        P(ALL, None),
        P(ROW, COL, None),
        P(),
        P(),
        P(ROW, COL, None, None, None),
        P(ROW, COL, None),
        P(ROW, COL, None),
        P(ROW, COL),
        P(ALL, None),
    )
    out_specs = (P(ALL, None), P(ALL, None), P(), P())
    return jax.shard_map(
        on_device, mesh=fine, in_specs=in_specs, out_specs=out_specs, check_vma=False
    )
```

```python
import functools

import jax
import jax.numpy as jnp
import numpy as np
from jax import lax
from jax.experimental import pallas as pl
from jax.experimental.pallas import tpu as pltpu
from jax.sharding import Mesh
from jax.sharding import PartitionSpec as P

TILE = 128
PER = 4
GROUP = 32
F32 = jnp.float32
BF16 = jnp.bfloat16
SIZES = {"y": 4, "xh": 2, "core": 2, "xl": 2, "z": 8}
ROW = ("y", "xh", "core")
COL = ("xl", "z")
ALL = ROW + COL


def permuted(x, axes, move):
    sizes = [SIZES[a] for a in axes]
    perm = []
    for i in range(int(np.prod(sizes))):
        to = move(np.unravel_index(i, sizes))
        perm.append((i, int(np.ravel_multi_index([t % s for t, s in zip(to, sizes)], sizes))))
    return lax.ppermute(x, axes, perm)


def shifted(x, axis, delta):
    return permuted(x, (axis,), lambda at: (at[0] + delta,))


def after(x, *others):
    return lax.optimization_barrier((x,) + others)[0]


def twin(x):
    return shifted(x, "core", 1)


def apart(x, axis, delta):
    axes = tuple(sorted(("core", axis), key=ALL.index))

    def move(at):
        place = dict(zip(axes, at))
        place[axis] += (1 - 2 * place["core"]) * delta
        return [place[a] for a in axes]

    return permuted(x, axes, move)


def one_hot_t(order_ref, nodes):
    here = lax.broadcasted_iota(jnp.int32, (nodes, nodes), 0)
    return (here == order_ref[...]).astype(BF16)


def dot(a, b, dims=((1,), (0,))):
    return lax.dot_general(a, b, (dims, ((), ())), preferred_element_type=F32)


def order_kernel(order_hbm, x_hbm, out_ref, order_ref, x_ref, sem):
    copies = [
        pltpu.make_async_copy(order_hbm, order_ref, sem.at[0]),
        pltpu.make_async_copy(x_hbm, x_ref, sem.at[1]),
    ]
    for c in copies:
        c.start()
    for c in copies:
        c.wait()
    pt = one_hot_t(order_ref, x_ref.shape[0])
    out_ref[...] = dot(pt, x_ref[...], ((0,), (0,))).astype(BF16)


def ordered_rows(order, x):
    anywhere = pl.BlockSpec(memory_space=pltpu.HBM)
    return pl.pallas_call(
        order_kernel,
        out_shape=jax.ShapeDtypeStruct(x.shape, x.dtype),
        in_specs=[anywhere] * 2,
        out_specs=pl.BlockSpec(memory_space=pltpu.VMEM),
        scratch_shapes=[
            pltpu.VMEM(order.shape, order.dtype),
            pltpu.VMEM(x.shape, x.dtype),
            pltpu.SemaphoreType.DMA((2,)),
        ],
        compiler_params=pltpu.CompilerParams(vmem_limit_bytes=32 << 20),
        name="order",
    )(order, x)


def tiles_kernel(transpose, spans, segments, *refs):
    count_ref, in_at, out_at, rows_hbm, cols_hbm, tiles_hbm = refs[:6]
    blocks = refs[6 : 6 + len(spans)]
    outs = refs[6 + len(spans) : -6]
    rows_ref, cols_ref, tiles, held, total, sem = refs[-6:]
    chunks = tiles_hbm.shape[2] // GROUP

    def load(c):
        at = pl.ds(c * GROUP, GROUP)
        return pltpu.make_async_copy(tiles_hbm.at[0, 0, at], tiles.at[at], sem.at[c])

    copies = [
        pltpu.make_async_copy(rows_hbm, rows_ref, sem.at[chunks]),
        pltpu.make_async_copy(cols_hbm, cols_ref, sem.at[chunks + 1]),
    ]
    for c in copies:
        c.start()
    for c in range(chunks):
        load(c).start()
    count = count_ref[0, 0]

    def zero(i, _):
        total[i] = jnp.zeros((TILE, TILE), F32)
        return 0

    lax.fori_loop(0, segments, zero, 0, unroll=4)
    for i, ((lo, n), b) in enumerate(zip(spans, blocks)):
        held[pl.ds(in_at[i], n)] = b[lo : lo + n]
    for c in copies:
        c.wait()

    def step(g, _):
        load(g).wait()
        products = []
        for u in range(GROUP):
            t = g * GROUP + u
            if transpose:
                products.append((cols_ref[0, 0, t], dot(held[rows_ref[0, 0, t]], tiles[t])))
            else:
                products.append((rows_ref[0, 0, t], dot(tiles[t], held[cols_ref[0, 0, t]])))
        for u, (target, product) in enumerate(products):
            target = jnp.where(g * GROUP + u < count, target, segments)
            total[target] += product
        return 0

    def unused(g, _):
        load(g).wait()
        return 0

    used = (count + GROUP - 1) // GROUP
    lax.fori_loop(0, used, step, 0)
    at = 0
    for out in outs:
        for k in range(0, out.shape[0], PER):
            out[pl.ds(k, PER)] = total[pl.ds(out_at[at], PER)].astype(BF16)
            at += 1
    lax.fori_loop(used, chunks, unused, 0)


def tile_sum(tiles, rows, cols, count, ins, outs, segments, transpose):
    slots = tiles.shape[2]
    smem = pl.BlockSpec(memory_space=pltpu.SMEM)
    hbm = pl.BlockSpec(memory_space=pltpu.HBM)
    vmem = pl.BlockSpec(memory_space=pltpu.VMEM)
    in_at = jnp.stack([i[0] for i in ins]).astype(jnp.int32)
    out_at = jnp.stack([at for out in outs for at in out]).astype(jnp.int32)
    return pl.pallas_call(
        functools.partial(tiles_kernel, transpose, [i[2:] for i in ins], segments),
        out_shape=[jax.ShapeDtypeStruct((len(o) * PER, TILE, TILE), BF16) for o in outs],
        in_specs=[smem] * 3 + [hbm] * 3 + [vmem] * len(ins),
        out_specs=[vmem] * len(outs),
        scratch_shapes=[
            pltpu.SMEM(rows.shape, jnp.int32),
            pltpu.SMEM(cols.shape, jnp.int32),
            pltpu.VMEM((slots, TILE, TILE), BF16),
            pltpu.VMEM((segments, TILE, TILE), BF16),
            pltpu.VMEM((segments + 1, TILE, TILE), F32),
            pltpu.SemaphoreType.DMA((slots // GROUP + 2,)),
        ],
        compiler_params=pltpu.CompilerParams(vmem_limit_bytes=40 << 20),
        cost_estimate=pl.CostEstimate(
            flops=2 * slots * TILE**3, bytes_accessed=slots * TILE * TILE * 2, transcendentals=0
        ),
        name="tile_sum_t" if transpose else "tile_sum",
    )(count, in_at, out_at, rows, cols, tiles, *[i[1] for i in ins])


def part_sum(offsets, parts):
    terms = [p[pl.ds(lo, PER)].astype(F32) for lo, p in zip(offsets, parts)]
    return functools.reduce(lambda a, b: a + b, terms)


def act_kernel(offsets, *refs):
    order_ref, cot_ref, weight_ref, bias_ref = refs[:4]
    parts = refs[4:-5]
    gt_ref, hi_ref, lo_ref, act_ref, bias_out = refs[-5:]
    nodes = cot_ref.shape[0]
    cot = dot(one_hot_t(order_ref, nodes), cot_ref[...], ((0,), (0,)))
    total = part_sum(offsets, parts).reshape(nodes, TILE)
    hi = total.astype(BF16)
    lo = (total - hi.astype(F32)).astype(BF16)
    hi_ref[...] = hi
    lo_ref[...] = lo
    weight = weight_ref[...]
    pre = dot(hi, weight) + dot(lo, weight) + bias_ref[...]
    sig = jax.nn.sigmoid(pre)
    grad = cot * (sig * (1.0 + pre * (1.0 - sig)))
    act_ref[...] = (pre * sig).astype(BF16)
    bias_out[...] = jnp.sum(grad, axis=0, keepdims=True)
    for t in range(nodes // TILE):
        gt_ref[t] = grad[t * TILE : (t + 1) * TILE].T.astype(BF16)


def side_kernel(order_ref, act_ref, gt_ref, hi_ref, lo_ref, bias_ref, out_ref, sums_ref):
    nodes = act_ref.shape[0]
    out_ref[...] = dot(one_hot_t(order_ref, nodes), act_ref[...]).astype(BF16)
    total = jnp.zeros((TILE, TILE), F32)
    for t in range(nodes // TILE):
        sl = pl.ds(t * TILE, TILE)
        total += dot(gt_ref[t], hi_ref[sl]) + dot(gt_ref[t], lo_ref[sl])
    sums_ref[:TILE] = total.T
    sums_ref[TILE:] = jnp.broadcast_to(bias_ref[...], (8, TILE))


def input_kernel(offsets, *refs):
    order_ref, weight_ref = refs[:2]
    parts = refs[2:-1]
    out_ref = refs[-1]
    nodes = out_ref.shape[0]
    total = part_sum(offsets, parts)
    grad = total.astype(BF16)
    back = jnp.concatenate(
        [dot(weight_ref[...], grad[t]).astype(BF16) for t in range(nodes // TILE)], axis=1
    )
    out_ref[...] = dot(one_hot_t(order_ref, nodes), back, ((1,), (1,))).astype(BF16)


def add_kernel(spans, *refs):
    parts, out = refs[:-1], refs[-1]
    for t in range(out.shape[0]):
        terms = [
            p[lo + t - at].astype(F32) for (at, lo, n), p in zip(spans, parts) if at <= t < at + n
        ]
        out[t] = functools.reduce(lambda a, b: a + b, terms).astype(out.dtype)


def added(tiles, *parts):
    return call(
        functools.partial(add_kernel, [(at, lo, n) for at, _, lo, n in parts]),
        jax.ShapeDtypeStruct((tiles,) + parts[0][1].shape[1:], parts[0][1].dtype),
        "add",
        *[p[1] for p in parts],
    )


def joined(*parts):
    at, spans = 0, []
    for a, lo, n in parts:
        spans.append((at, a, lo, n))
        at += n
    return added(at, *spans)


def call(kernel, out_shape, name, *args):
    vmem = pl.BlockSpec(memory_space=pltpu.VMEM)
    return pl.pallas_call(
        kernel,
        out_shape=out_shape,
        in_specs=[vmem] * len(args),
        out_specs=jax.tree.map(lambda _: vmem, out_shape),
        compiler_params=pltpu.CompilerParams(vmem_limit_bytes=32 << 20),
        name=name,
    )(*args)


def shape(*dims, dtype=BF16):
    return jax.ShapeDtypeStruct(dims, dtype)


def gather_row_b(mine, place, core, up):
    n = PER
    other = twin(mine)
    both = joined((mine, 0, n), (other, 0, n))
    side = shifted(mine, "xh", 1)
    near = apart(both, "y", 1)
    far = shifted(mine, "y", 2)
    side_other = twin(side)
    side_near = apart(joined((side, 0, n), (side_other, 0, n)), "y", 1)
    side_far = shifted(far, "xh", 1)
    out = []

    def put(a, dy, dx, c, lo=0):
        out.append((place(ROW, (dy, dx, c)), a, lo, n))

    for dx, own, own_t, a, b in ((0, mine, other, near, far), (1, side, side_other, side_near, side_far)):
        put(own, 0, dx, 0)
        put(own_t, 0, dx, 1)
        a_t = twin(a)
        put(a, -up, dx, 0)
        put(a, -up, dx, 1, n)
        put(a_t, up, dx, 1)
        put(a_t, up, dx, 0, n)
        put(b, 2, dx, 0)
        put(twin(b), 2, dx, 1)
    return out


def row_targets_b(place, core, up):
    def at(dy, dx, c):
        return place(ROW, (dy, dx, c))

    return [
        [at(-up, 0, 1), at(-up, 1, 1), at(-up, 0, 0), at(-up, 1, 0)],
        [at(2, 1, 1), at(2, 0, 1), at(0, 1, 1), at(0, 0, 1)],
        [at(up, 0, 0), at(up, 1, 0), at(up, 0, 1), at(up, 1, 1)],
        [at(2, 1, 0), at(2, 0, 0), at(0, 1, 0), at(0, 0, 0)],
    ]


def scatter_row_b(pieces, hook):
    n = PER
    near_t, rest_t, near, rest = pieces
    near_t, rest_t = twin(near_t), twin(rest_t)
    near = apart(added(4 * n, (0, near, 0, 4 * n), (0, near_t, 0, 4 * n)), "y", 1)
    corner = shifted(added(n, (0, rest, 0, n), (0, rest_t, 0, n)), "xh", 1)
    hook(corner)
    near_t = twin(near[2 * n :])
    far = shifted(added(n, (0, rest, n, n), (0, rest_t, n, n), (0, corner, 0, n)), "y", 2)
    side = added(
        n, (0, rest, 2 * n, n), (0, rest_t, 2 * n, n), (0, near, n, n), (0, near_t, n, n)
    )
    side = shifted(side, "xh", 1)
    return [(rest, 3 * n), (rest_t, 3 * n), (near, 0), (near_t, 0), (far, 0), (side, 0)]


def gather_col_b(mine, place, up, hook):
    n = PER
    other = twin(mine)
    x_own = shifted(mine, "xl", 1)
    hook(x_own)
    both = joined((mine, 0, n), (other, 0, n))
    two = apart(both, "z", 2)
    one = apart(both, "z", 1)
    x_one = apart(joined((x_own, 0, n), (twin(x_own), 0, n)), "z", 1)
    three = apart(two, "z", 1)
    four = apart(two[:n], "z", 2)
    x_two = shifted(two, "xl", 1)
    x_three = shifted(three, "xl", 1)
    x_four = shifted(four, "xl", 1)
    out = []
    for dx, own, steps, last in (
        (0, mine, (one, two, three), four),
        (1, x_own, (x_one, x_two, x_three), x_four),
    ):
        out.append((place(COL, (dx, 0)), own, 0, n))
        for d, a in enumerate(steps, 1):
            out.append((place(COL, (dx, -up * d)), a, 0, n))
            out.append((place(COL, (dx, up * d)), twin(a[n:]), 0, n))
        out.append((place(COL, (dx, 4)), last, 0, n))
    return out


def col_targets_b(place, up):
    def at(dx, d):
        return place(COL, (dx, up * d))

    return [
        [at(1, -3), at(1, -2)],
        [at(1, -1), at(0, -1), at(0, -2), at(0, -3)],
        [at(1, 3)],
        [at(1, 2)],
        [at(1, 1), at(0, 1)],
        [at(0, 2)],
        [at(0, 3)],
        [at(1, 4)],
        [at(0, 4)],
        [at(1, 0)],
        [at(0, 0)],
    ]


def scatter_col_b(pieces):
    n = PER
    x_t, rest_t, x_three, x_two, near, two, three, x_four, four, x_own, own = pieces
    x_t, rest_t = twin(x_t), twin(rest_t)
    x_three = shifted(joined((x_three, 0, n), (x_t, 0, n)), "xl", 1)
    x_four = shifted(x_four, "xl", 1)
    x_two = shifted(joined((x_two, 0, n), (x_t, n, n)), "xl", 1)
    near = apart(joined((near, 0, 2 * n), (rest_t, 0, 2 * n)), "z", 1)
    three = added(2 * n, (0, three, 0, n), (n, rest_t, 3 * n, n), (0, x_three, 0, 2 * n))
    three = apart(three, "z", 1)
    four = apart(added(n, (0, four, 0, n), (0, x_four, 0, n)), "z", 2)
    near_t = twin(near[2 * n :])
    side = shifted(added(n, (0, x_own, 0, n), (0, near, 0, n), (0, near_t, 0, n)), "xl", 1)
    two = added(
        2 * n,
        (0, two, 0, n),
        (n, rest_t, 2 * n, n),
        (0, x_two, 0, 2 * n),
        (0, three, 0, 2 * n),
        (0, four, 0, n),
    )
    two = apart(two, "z", 2)
    return [(own, 0), (near, n), (near_t, n), (side, 0), (two, 0), (twin(two[n:]), 0)]


def gather_row_a(mine, place, core, up):
    n = PER
    near = {(0, 0): mine}
    for dy in (2, 1, -1):
        near[dy, 0] = shifted(mine, "y", dy)
    near[0, 1] = shifted(mine, "xh", 1)
    near[2, 1] = shifted(near[2, 0], "xh", 1)
    for dy in (1, -1):
        near[dy, 1] = shifted(near[0, 1], "y", dy)
    out = []
    for (dy, dx), b in near.items():
        out.append((place(ROW, (-dy, -dx, 0)), b, 0, n))
        out.append((place(ROW, (-dy, -dx, 1)), twin(b), 0, n))
    return out


def gather_row_c(mine, place, core, up):
    n = PER
    far = shifted(mine, "y", 2)
    corner = permuted(mine, ("y", "xh"), lambda at: (at[0] + 2, at[1] + 1))
    side = shifted(mine, "xh", 1)
    other = twin(mine)
    both = joined((mine, 0, n), (other, 0, n))
    near = apart(both, "y", 1)
    axes = ("y", "xh", "core")
    slant = permuted(both, axes, lambda at: (at[0] + 1 - 2 * at[2], at[1] + 1, at[2]))
    out = []

    def put(a, dy, dx, c, lo=0):
        out.append((place(ROW, (dy, dx, c)), a, lo, n))

    for dx, own, own_t, a, b in (
        (0, mine, other, near, far),
        (1, side, None, slant, corner),
    ):
        put(own, 0, dx, 0)
        put(twin(own) if own_t is None else own_t, 0, dx, 1)
        a_t = twin(a)
        put(a, -up, dx, 0)
        put(a, -up, dx, 1, n)
        put(a_t, up, dx, 1)
        put(a_t, up, dx, 0, n)
        put(b, 2, dx, 0)
        put(twin(b), 2, dx, 1)
    return out


ROW_ORDER = [(2, 1), (1, 1), (-1, 1), (2, 0), (0, 1), (1, 0), (-1, 0), (0, 0)]


def row_targets_a(place, core, up):
    return [[place(ROW, d + (c,))] for c in (0, 1) for d in ROW_ORDER]


def scatter_row_a(pieces, hook):
    n = PER
    mine, theirs = pieces[:8], pieces[8:]
    got = [twin(t) for t in theirs]
    far, up, down, two, side, one, back, own = [
        added(n, (0, a, 0, n), (0, b, 0, n)) for a, b in zip(mine, got)
    ]
    far = shifted(far, "xh", 1)
    up, down = shifted(up, "y", 1), shifted(down, "y", -1)
    two = shifted(added(n, (0, two, 0, n), (0, far, 0, n)), "y", 2)
    one, back = shifted(one, "y", 1), shifted(back, "y", -1)
    side = shifted(added(n, (0, side, 0, n), (0, up, 0, n), (0, down, 0, n)), "xh", 1)
    return [(own, 0), (one, 0), (back, 0), (two, 0), (side, 0)]


def gather_col_a(mine, place, up, hook):
    n, half = PER, PER // 2
    z = {0: mine}
    for d in (2, -2):
        z[d] = shifted(mine, "z", d)
    x = {0: shifted(mine, "xl", 1)}
    hook(x[0])
    for d in (1, -1):
        z[d] = shifted(mine, "z", d)
    z[3] = shifted(z[2], "z", 1)
    z[-3] = shifted(z[-2], "z", -1)
    low = shifted(z[2][:half], "z", 2)
    high = shifted(z[-2][half:], "z", -2)
    for d in (1, -1):
        x[d] = shifted(x[0], "z", d)
    for d in (2, -2, 3, -3):
        x[d] = shifted(z[d], "xl", 1)
    out = [(place(COL, (0, -d)), b, 0, n) for d, b in z.items()]
    out += [(place(COL, (1, -d)), b, 0, n) for d, b in x.items()]
    for dx, a, b in ((0, low, high), (1, shifted(low, "xl", 1), shifted(high, "xl", 1))):
        at = place(COL, (dx, 4))
        out += [(at, a, 0, half), (at + half, b, 0, half)]
    return out


COL_ORDER = (4, 3, -3, 2, -2, 1, -1, 0)


def col_targets_a(place, up):
    return [[place(COL, (x, d))] for x in (0, 1) for d in COL_ORDER]


def scatter_col_a(pieces):
    n, half = PER, PER // 2
    o = dict(zip(COL_ORDER, pieces[:8]))
    t = dict(zip(COL_ORDER, pieces[8:]))
    r = {d: shifted(t[d], "xl", 1) for d in (4, 3, -3, 2, -2)}
    near = [shifted(t[d], "z", d) for d in (1, -1)]
    last = [shifted(o[d], "z", d) for d in (1, -1)]
    low = added(half, (0, o[4], 0, half), (0, r[4], 0, half))
    high = added(half, (0, o[4], half, half), (0, r[4], half, half))
    fours = {2: (0, shifted(low, "z", 2), 0, half), -2: (half, shifted(high, "z", -2), 0, half)}
    threes = {
        2 * s: shifted(added(n, (0, o[3 * s], 0, n), (0, r[3 * s], 0, n)), "z", s)
        for s in (1, -1)
    }
    twos = [
        shifted(
            added(n, (0, o[d], 0, n), (0, r[d], 0, n), (0, threes[d], 0, n), fours[d]), "z", d
        )
        for d in (2, -2)
    ]
    side = shifted(added(n, (0, t[0], 0, n), *[(0, a, 0, n) for a in near]), "xl", 1)
    return [(a, 0) for a in [o[0], side] + last + twos]


def reduce_over(x, axis, bit):
    other = permuted(x, (axis,), lambda at: (at[0] ^ bit,))
    n = x.shape[0]
    return added(n, (0, x, 0, n), (0, other, 0, n))


def on_device(
    features, node_order, weight, bias, tile_values, tile_rows, tile_cols, tile_count, cotangent
):
    nodes, width = features.shape
    order = node_order.reshape(1, nodes)
    tiles = tile_values
    me = {a: lax.axis_index(a) for a in ALL}

    def place(axes, delta):
        at = 0
        for a, d in zip(axes, delta):
            at = at * SIZES[a] + lax.rem(me[a] + d + SIZES[a], SIZES[a])
        return at * PER

    core, up = me["core"], 1 - 2 * me["core"]

    row_tiles = SIZES["xl"] * SIZES["z"] * PER
    col_tiles = SIZES["y"] * SIZES["xh"] * SIZES["core"] * PER
    ordered = ordered_rows(order, features).reshape(PER, TILE, width)
    pieces = tile_sum(
        tiles,
        tile_rows,
        tile_cols,
        tile_count,
        gather_row_a(ordered, place, core, up),
        col_targets_a(place, up),
        row_tiles,
        False,
    )
    parts = scatter_col_a(pieces)
    gt, hi, lo, act, bias_part = call(
        functools.partial(act_kernel, [p[1] for p in parts]),
        [shape(PER, TILE, TILE)] + [shape(nodes, width)] * 3 + [shape(1, width, dtype=F32)],
        "act",
        order,
        cotangent,
        weight,
        bias.reshape(1, width),
        *[p[0] for p in parts],
    )
    tokens = []
    gs = gather_col_a(gt, place, up, tokens.append)
    activated, sums = call(
        side_kernel,
        [shape(nodes, width), shape(width + 8, width, dtype=F32)],
        "side",
        order,
        after(act, *tokens),
        gt,
        hi,
        lo,
        bias_part,
    )
    sums = sums.reshape(-1, 8, width)
    for axis, bit in (("core", 1), ("xh", 1), ("y", 1), ("y", 2), ("xl", 1)):
        sums = reduce_over(sums, axis, bit)
    pieces = tile_sum(
        tiles,
        tile_rows,
        tile_cols,
        tile_count,
        gs,
        row_targets_a(place, core, up),
        col_tiles,
        True,
    )
    tokens = []
    parts = scatter_row_a(pieces, tokens.append)
    for bit in (1, 2, 4):
        sums = reduce_over(after(sums, *tokens), "z", bit)
    sums = sums.reshape(-1, width)
    weight_grad, bias_grad = sums[:width], sums[width]
    input_grad = call(
        functools.partial(input_kernel, [p[1] for p in parts]),
        shape(nodes, width),
        "input",
        order,
        weight,
        *[p[0] for p in parts],
    )
    return activated, input_grad, weight_grad, bias_grad


def solution(mesh):
    fine = Mesh(mesh.devices.reshape([SIZES[a] for a in ALL]), ALL)
    in_specs = (
        P(ALL, None),
        P(ROW, COL, None),
        P(),
        P(),
        P(ROW, COL, None, None, None),
        P(ROW, COL, None),
        P(ROW, COL, None),
        P(ROW, COL),
        P(ALL, None),
    )
    out_specs = (P(ALL, None), P(ALL, None), P(), P())
    return jax.shard_map(
        on_device, mesh=fine, in_specs=in_specs, out_specs=out_specs, check_vma=False
    )
```

```python
import functools

import jax
import jax.numpy as jnp
import numpy as np
from jax import lax
from jax.experimental import pallas as pl
from jax.experimental.pallas import tpu as pltpu
from jax.sharding import Mesh
from jax.sharding import PartitionSpec as P

TILE = 128
PER = 4
ROWS = PER * TILE
EXTRA = TILE + 16
GROUP = 32
F32 = jnp.float32
BF16 = jnp.bfloat16
SIZES = {"y": 4, "xh": 2, "core": 2, "xl": 2, "z": 8}
ROW = ("y", "xh", "core")
COL = ("xl", "z")
ALL = ROW + COL


def permuted(x, axes, move):
    if x is None:
        return None
    sizes = [SIZES[a] for a in axes]
    perm = []
    for i in range(int(np.prod(sizes))):
        to = move(np.unravel_index(i, sizes))
        perm.append((i, int(np.ravel_multi_index([t % s for t, s in zip(to, sizes)], sizes))))
    return lax.ppermute(x, axes, perm)


def shifted(x, axis, delta):
    return permuted(x, (axis,), lambda at: (at[0] + delta,))


def after(x, *others):
    return lax.optimization_barrier((x,) + others)[0]


def twin(x):
    return shifted(x, "core", 1)


def apart(x, axes, delta):
    def move(at):
        place = dict(zip(axes, at))
        return [place[a] + d * (1 - 2 * place["core"] if a == "y" else 1) for a, d in zip(axes, delta)]

    return permuted(x, axes, move)


def one_hot_t(order_ref, nodes):
    here = lax.broadcasted_iota(jnp.int32, (nodes, nodes), 0)
    return (here == order_ref[...]).astype(BF16)


def dot(a, b, dims=((1,), (0,))):
    return lax.dot_general(a, b, (dims, ((), ())), preferred_element_type=F32)


def summed(terms):
    return functools.reduce(lambda a, b: a + b, terms)


def tiles_kernel(transpose, spans, plan_at, segments, *refs):
    plan, tiles_hbm = refs[:2]
    blocks = refs[2 : 2 + len(spans)]
    outs = refs[2 + len(spans) : -4]
    tiles, held, total, sem = refs[-4:]
    slots = tiles_hbm.shape[2]
    chunks = slots // GROUP

    def load(c):
        at = pl.ds(c * GROUP, GROUP)
        return pltpu.make_async_copy(tiles_hbm.at[0, 0, at], tiles.at[at], sem.at[c])

    for c in range(chunks):
        load(c).start()
    count = plan[0]

    def zero(i, _):
        total[i] = jnp.zeros((TILE, TILE), F32)
        return 0

    lax.fori_loop(0, segments, zero, 0, unroll=4)
    for i, ((lo, n), b) in enumerate(zip(spans, blocks)):
        held[pl.ds(plan[plan_at + i], n // TILE)] = b[lo : lo + n].reshape(n // TILE, TILE, TILE)

    def step(g, _):
        load(g).wait()
        products = []
        for u in range(GROUP):
            t = g * GROUP + u
            if transpose:
                products.append((plan[1 + slots + t], dot(held[plan[1 + t]], tiles[t])))
            else:
                products.append((plan[1 + t], dot(tiles[t], held[plan[1 + slots + t]])))
        for u, (target, product) in enumerate(products):
            target = jnp.where(g * GROUP + u < count, target, segments)
            total[target] += product
        return 0

    def unused(g, _):
        load(g).wait()
        return 0

    used = (count + GROUP - 1) // GROUP
    lax.fori_loop(0, used, step, 0)
    at = plan_at + len(spans)
    for out in outs:
        for k in range(0, out.shape[0], ROWS):
            block = total[pl.ds(plan[at], PER)].astype(BF16)
            out[pl.ds(k, ROWS)] = block.reshape(ROWS, TILE)
            at += 1
    lax.fori_loop(used, chunks, unused, 0)


def tile_sum(tiles, plan, plan_at, ins, outs, segments, transpose):
    slots = tiles.shape[2]
    vmem = pl.BlockSpec(memory_space=pltpu.VMEM)
    return pl.pallas_call(
        functools.partial(tiles_kernel, transpose, [i[1:] for i in ins], plan_at, segments),
        out_shape=[shape(n * ROWS, TILE) for n in outs],
        in_specs=[pl.BlockSpec(memory_space=pltpu.SMEM), pl.BlockSpec(memory_space=pltpu.HBM)]
        + [vmem] * len(ins),
        out_specs=[vmem] * len(outs),
        scratch_shapes=[
            pltpu.VMEM((slots, TILE, TILE), BF16),
            pltpu.VMEM((segments, TILE, TILE), BF16),
            pltpu.VMEM((segments + 1, TILE, TILE), F32),
            pltpu.SemaphoreType.DMA((slots // GROUP,)),
        ],
        compiler_params=pltpu.CompilerParams(vmem_limit_bytes=40 << 20),
        cost_estimate=pl.CostEstimate(
            flops=2 * slots * TILE**3, bytes_accessed=slots * TILE * TILE * 2, transcendentals=0
        ),
        name="tile_sum_t" if transpose else "tile_sum",
    )(plan, tiles, *[i[0] for i in ins])


def packed(weight, bias):
    high = bias.astype(BF16)
    low = (bias - high.astype(F32)).astype(BF16)
    rest = jnp.zeros((EXTRA - TILE - 2, TILE), BF16)
    return jnp.concatenate([weight.astype(BF16), high, low, rest], axis=0)


def unpacked(rows):
    rows = rows.astype(F32)
    return rows[:TILE], rows[TILE : TILE + 1] + rows[TILE + 1 : TILE + 2]


def total_of(offsets, parts):
    return summed([p[lo : lo + ROWS].astype(F32) for lo, p in zip(offsets, parts)])


def act_kernel(offsets, *refs):
    order_ref, cot_ref, weight_ref, bias_ref = refs[:4]
    parts = refs[4:-2]
    out_ref, act_ref = refs[-2:]
    nodes = cot_ref.shape[0]
    cot = dot(one_hot_t(order_ref, nodes), cot_ref[...], ((0,), (0,)))
    total = total_of(offsets, parts)
    hi = total.astype(BF16)
    lo = (total - hi.astype(F32)).astype(BF16)
    weight = weight_ref[...]
    pre = dot(hi, weight) + dot(lo, weight) + bias_ref[...]
    sig = jax.nn.sigmoid(pre)
    grad = cot * (sig * (1.0 + pre * (1.0 - sig)))
    act_ref[...] = (pre * sig).astype(BF16)
    weight_grad = jnp.zeros((TILE, TILE), F32)
    for t in range(0, nodes, TILE):
        grad_t = grad[t : t + TILE].T.astype(BF16)
        out_ref[t : t + TILE] = grad_t
        weight_grad += dot(grad_t, hi[t : t + TILE]) + dot(grad_t, lo[t : t + TILE])
    out_ref[nodes:] = packed(weight_grad, jnp.sum(grad, axis=0, keepdims=True))


def restore_kernel(order_ref, act_ref, out_ref):
    out_ref[...] = dot(one_hot_t(order_ref, act_ref.shape[0]), act_ref[...]).astype(BF16)


def input_kernel(offsets, *refs):
    order_ref, weight_ref = refs[:2]
    parts = refs[2:-1]
    out_ref = refs[-1]
    nodes = out_ref.shape[0]
    grad = total_of(offsets, parts).astype(BF16)
    back = jnp.concatenate(
        [dot(weight_ref[...], grad[t : t + TILE]).astype(BF16) for t in range(0, nodes, TILE)],
        axis=1,
    )
    out_ref[...] = dot(one_hot_t(order_ref, nodes), back, ((1,), (1,))).astype(BF16)


def add_kernel(spans, *refs):
    parts, out = refs[:-1], refs[-1]
    cuts = sorted({c for at, _, n in spans for c in (at, at + n)})
    for a, b in zip(cuts, cuts[1:]):
        terms = [
            p[lo + a - at : lo + b - at].astype(F32)
            for (at, lo, n), p in zip(spans, parts)
            if at <= a and b <= at + n
        ]
        out[a:b] = summed(terms).astype(out.dtype)


def added(rows, *parts):
    return call(
        functools.partial(add_kernel, [(at, lo, n) for at, _, lo, n in parts]),
        shape(rows, TILE),
        "add",
        *[p[1] for p in parts],
    )


def joined(*parts):
    if parts[0][0] is None:
        return None
    at, spans = 0, []
    for a, lo, n in parts:
        spans.append((at, a, lo, n))
        at += n
    return added(at, *spans)


def slab_kernel(offsets, plan_at, *refs):
    plan, parts, outs, held = refs[0], refs[1 : 1 + len(offsets)], refs[1 + len(offsets) : -1], refs[-1]
    for i, (lo, p) in enumerate(zip(offsets, parts)):
        held[plan[plan_at + i]] = p[lo : lo + EXTRA]
    pairs = [unpacked(held[i]) for i in range(len(offsets))]
    weight, bias = summed([p[0] for p in pairs]), summed([p[1] for p in pairs])
    if len(outs) == 1:
        outs[0][...] = packed(weight, bias)
    else:
        outs[0][...] = weight.T
        outs[1][...] = bias


def slab_sum(plan, plan_at, parts, out_shape):
    vmem = pl.BlockSpec(memory_space=pltpu.VMEM)
    return pl.pallas_call(
        functools.partial(slab_kernel, [p[1] for p in parts], plan_at),
        out_shape=out_shape,
        in_specs=[pl.BlockSpec(memory_space=pltpu.SMEM)] + [vmem] * len(parts),
        out_specs=[vmem] * len(out_shape),
        scratch_shapes=[pltpu.VMEM((len(parts), EXTRA, TILE), BF16)],
        compiler_params=pltpu.CompilerParams(vmem_limit_bytes=32 << 20),
        name="slab",
    )(plan, *[p[0] for p in parts])


def chip_kernel(a_ref, b_ref, out_ref):
    (weight_a, bias_a), (weight_b, bias_b) = unpacked(a_ref[...]), unpacked(b_ref[...])
    out_ref[...] = packed(weight_a + weight_b, bias_a + bias_b)


def call(kernel, out_shape, name, *args):
    vmem = pl.BlockSpec(memory_space=pltpu.VMEM)
    return pl.pallas_call(
        kernel,
        out_shape=out_shape,
        in_specs=[vmem] * len(args),
        out_specs=jax.tree.map(lambda _: vmem, out_shape),
        compiler_params=pltpu.CompilerParams(vmem_limit_bytes=32 << 20),
        name=name,
    )(*args)


def shape(*dims, dtype=BF16):
    return jax.ShapeDtypeStruct(dims, dtype)


def gather_row(mine, place, up, plan=None):
    n = ROWS
    near = {(0, 0): mine}
    for dy in (2, 1, -1):
        near[dy, 0] = shifted(mine, "y", dy)
    near[0, 1] = shifted(mine, "xh", 1)
    near[2, 1] = shifted(near[2, 0], "xh", 1)
    if plan is not None:
        near[0, 1] = after(near[0, 1], plan)
    for dy in (1, -1):
        near[dy, 1] = shifted(near[0, 1], "y", dy)
    out = []
    for (dy, dx), b in near.items():
        out.append((place(ROW, (-dy, -dx, 0)), b, 0, n))
        out.append((place(ROW, (-dy, -dx, 1)), twin(b), 0, n))
    return out


COL_ORDER = (4, 3, -3, 2, -2, 1, -1, 0)


def col_targets(place):
    return [[place(COL, (x, d))] for x in (0, 1) for d in COL_ORDER]


def scatter_col(pieces):
    n, half = ROWS, ROWS // 2
    o = dict(zip(COL_ORDER, pieces[:8]))
    t = dict(zip(COL_ORDER, pieces[8:]))
    r = {d: shifted(t[d], "xl", 1) for d in (4, 3, -3, 2, -2)}
    near = [shifted(t[d], "z", d) for d in (1, -1)]
    last = [shifted(o[d], "z", d) for d in (1, -1)]
    low = added(half, (0, o[4], 0, half), (0, r[4], 0, half))
    high = added(half, (0, o[4], half, half), (0, r[4], half, half))
    fours = {2: (0, shifted(low, "z", 2), 0, half), -2: (half, shifted(high, "z", -2), 0, half)}
    threes = {
        2 * s: shifted(added(n, (0, o[3 * s], 0, n), (0, r[3 * s], 0, n)), "z", s)
        for s in (1, -1)
    }
    twos = [
        shifted(
            added(n, (0, o[d], 0, n), (0, r[d], 0, n), (0, threes[d], 0, n), fours[d]), "z", d
        )
        for d in (2, -2)
    ]
    side = shifted(added(n, (0, t[0], 0, n), *[(0, a, 0, n) for a in near]), "xl", 1)
    return [(a, 0) for a in [o[0], side] + last + twos]


def gather_col(mine, place, hook=None):
    n, half = ROWS, ROWS // 2
    z = {0: mine}
    for d in (2, -2):
        z[d] = shifted(mine, "z", d)
    x = {0: shifted(mine, "xl", 1)}
    if hook is not None:
        hook(x[0])
    for d in (1, -1):
        z[d] = shifted(mine, "z", d)
    z[3] = shifted(z[2], "z", 1)
    z[-3] = shifted(z[-2], "z", -1)
    low = high = None
    if mine is not None:
        low, high = z[2][:half], z[-2][half:]
    low, high = shifted(low, "z", 2), shifted(high, "z", -2)
    for d in (1, -1):
        x[d] = shifted(x[0], "z", d)
    for d in (2, -2, 3, -3):
        x[d] = shifted(z[d], "xl", 1)
    blocks = [((0, -d), b) for d, b in z.items()] + [((1, -d), b) for d, b in x.items()]
    out = [(place(COL, at), b, 0, n) for at, b in blocks]
    extra = [(place(COL, at), b, n) for at, b in blocks]
    for dx, a, b in ((0, low, high), (1, shifted(low, "xl", 1), shifted(high, "xl", 1))):
        at = place(COL, (dx, 4))
        out += [(at, a, 0, half), (at + PER // 2, b, 0, half)]
        extra.append((at, b, half))
    return out, extra


def row_targets(place):
    def at(c, *chips):
        return [place(ROW, chip + (c,)) for chip in chips]

    up, down = ((1, 1), (1, 0)), ((-1, 1), (-1, 0))
    rest = ((2, 1), (2, 0), (0, 1), (0, 0))
    return [at(1, *up, *down), at(1, *rest), at(0, *up), at(0, *down), at(0, *rest)]


CHIPS = ((0, 0), (-1, 0), (1, 0), (0, 1), (2, 0), (2, 1), (-1, 1), (1, 1))


def scatter_row(pieces, sums):
    n, e = ROWS, EXTRA
    near_t, rest_t, up, down, rest = pieces
    near_t, rest_t = twin(near_t), twin(rest_t)
    up = added(2 * n + e, (0, up, 0, 2 * n), (0, near_t, 0, 2 * n), (2 * n, sums, 0, e))
    up = shifted(up, "y", 1)
    down = added(2 * n + e, (0, down, 0, 2 * n), (0, near_t, 2 * n, 2 * n), (2 * n, sums, 0, e))
    down = shifted(down, "y", -1)
    corner = added(n + e, (0, rest, 0, n), (0, rest_t, 0, n), (n, sums, 0, e))
    corner = shifted(corner, "xh", 1)
    far = added(
        n + 2 * e,
        (0, rest, n, n),
        (0, rest_t, n, n),
        (0, corner, 0, n),
        (n, sums, 0, e),
        (n + e, corner, n, e),
    )
    far = shifted(far, "y", 2)
    side = added(
        n + 2 * e,
        (0, rest, 2 * n, n),
        (0, rest_t, 2 * n, n),
        (0, up, 0, n),
        (0, down, 0, n),
        (n, up, 2 * n, e),
        (n + e, down, 2 * n, e),
    )
    side = shifted(side, "xh", 1)
    parts = [(rest, 3 * n), (rest_t, 3 * n), (up, n), (down, n), (far, 0), (side, 0)]
    extra = [(sums, 0), (up, 2 * n), (down, 2 * n), (corner, n)]
    return parts, extra + [(a, at) for a in (far, side) for at in (n, n + e)]


def on_device(
    features, node_order, weight, bias, tile_values, tile_rows, tile_cols, tile_count, cotangent
):
    nodes, width = features.shape
    order = node_order.reshape(1, nodes)
    me = {a: lax.axis_index(a) for a in ALL}
    up = 1 - 2 * me["core"]

    def place(axes, delta):
        at = 0
        for a, d in zip(axes, delta):
            at = at * SIZES[a] + lax.rem(me[a] + d + SIZES[a], SIZES[a])
        return at * PER

    slab_tiles = SIZES["xl"] * SIZES["z"] * PER
    col_blocks, col_extra = gather_col(None, place)
    sections = [
        [h[0] for h in gather_row(None, place, up)] + [at for out in col_targets(place) for at in out],
        [h[0] for h in col_blocks] + [at for out in row_targets(place) for at in out],
        [h[0] // PER for h in col_extra],
        [place(("y", "xh"), d) // PER for d in CHIPS],
    ]
    numbers = [tile_count.reshape(1), tile_rows.reshape(-1), tile_cols.reshape(-1)]
    plan_at = [1 + 2 * tile_values.shape[2]]
    for here in sections:
        numbers.append(jnp.stack(here).astype(jnp.int32))
        plan_at.append(plan_at[-1] + len(here))
    plan = jnp.concatenate(numbers)

    ordered = features.at[order[0]].get(mode="promise_in_bounds")
    pieces = tile_sum(
        tile_values,
        plan,
        plan_at[0],
        [h[1:] for h in gather_row(ordered, place, up, plan)],
        [len(o) for o in col_targets(place)],
        slab_tiles,
        False,
    )
    parts = scatter_col(pieces)
    block, act = call(
        functools.partial(act_kernel, [p[1] for p in parts]),
        [shape(nodes + EXTRA, width), shape(nodes, width)],
        "act",
        order,
        cotangent,
        weight,
        bias.reshape(1, width),
        *[p[0] for p in parts],
    )
    tokens = []
    blocks, extra = gather_col(block, place, tokens.append)
    activated = call(
        restore_kernel, shape(nodes, width), "restore", order, after(act, *tokens)
    )
    (sums,) = slab_sum(plan, plan_at[2], [e[1:] for e in extra], [shape(EXTRA, width)])
    sums = call(chip_kernel, shape(EXTRA, width), "chip", sums, twin(sums))
    pieces = tile_sum(
        tile_values,
        plan,
        plan_at[1],
        [b[1:] for b in blocks],
        [len(o) for o in row_targets(place)],
        slab_tiles,
        True,
    )
    parts, extra = scatter_row(pieces, sums)
    input_grad = call(
        functools.partial(input_kernel, [p[1] for p in parts]),
        shape(nodes, width),
        "input",
        order,
        weight,
        *[p[0] for p in parts],
    )
    weight_grad, bias_grad = slab_sum(
        plan,
        plan_at[3],
        extra,
        [shape(width, width, dtype=F32), shape(1, width, dtype=F32)],
    )
    return activated, input_grad, weight_grad, bias_grad.reshape(width)


def solution(mesh):
    fine = Mesh(mesh.devices.reshape([SIZES[a] for a in ALL]), ALL)
    in_specs = (
        P(ALL, None),
        P(ROW, COL, None),
        P(),
        P(),
        P(ROW, COL, None, None, None),
        P(ROW, COL, None),
        P(ROW, COL, None),
        P(ROW, COL),
        P(ALL, None),
    )
    out_specs = (P(ALL, None), P(ALL, None), P(), P())
    return jax.shard_map(
        on_device, mesh=fine, in_specs=in_specs, out_specs=out_specs, check_vma=False
    )
```

```python
import functools

import jax
import jax.numpy as jnp
import numpy as np
from jax import lax
from jax.experimental import pallas as pl
from jax.experimental.pallas import tpu as pltpu
from jax.sharding import Mesh
from jax.sharding import PartitionSpec as P

TILE = 128
PER = 4
ROWS = PER * TILE
EXTRA = TILE + 16
GROUP = 32
F32 = jnp.float32
BF16 = jnp.bfloat16
SIZES = {"y": 4, "xh": 2, "core": 2, "xl": 2, "z": 8}
ROW = ("y", "xh", "core")
COL = ("xl", "z")
ALL = ROW + COL


def permuted(x, axes, move):
    if x is None:
        return None
    sizes = [SIZES[a] for a in axes]
    perm = []
    for i in range(int(np.prod(sizes))):
        to = move(np.unravel_index(i, sizes))
        perm.append((i, int(np.ravel_multi_index([t % s for t, s in zip(to, sizes)], sizes))))
    return lax.ppermute(x, axes, perm)


def shifted(x, axis, delta):
    return permuted(x, (axis,), lambda at: (at[0] + delta,))


def after(x, *others):
    return lax.optimization_barrier((x,) + others)[0]


def twin(x):
    return shifted(x, "core", 1)


def apart(x, axes, delta):
    def move(at):
        place = dict(zip(axes, at))
        return [place[a] + d * (1 - 2 * place["core"] if a == "y" else 1) for a, d in zip(axes, delta)]

    return permuted(x, axes, move)


def one_hot_t(order_ref, nodes):
    here = lax.broadcasted_iota(jnp.int32, (nodes, nodes), 0)
    return (here == order_ref[...]).astype(BF16)


def dot(a, b, dims=((1,), (0,))):
    return lax.dot_general(a, b, (dims, ((), ())), preferred_element_type=F32)


def summed(terms):
    return functools.reduce(lambda a, b: a + b, terms)


def tiles_kernel(transpose, spans, plan_at, segments, *refs):
    plan, tiles_hbm = refs[:2]
    blocks = refs[2 : 2 + len(spans)]
    outs = refs[2 + len(spans) : -4]
    tiles, held, total, sem = refs[-4:]
    slots = tiles_hbm.shape[2]
    chunks = slots // GROUP

    def load(c):
        at = pl.ds(c * GROUP, GROUP)
        return pltpu.make_async_copy(tiles_hbm.at[0, 0, at], tiles.at[at], sem.at[c])

    for c in range(chunks):
        load(c).start()
    count = plan[0]

    def zero(i, _):
        total[i] = jnp.zeros((TILE, TILE), F32)
        return 0

    lax.fori_loop(0, segments, zero, 0, unroll=4)
    for i, ((lo, n), b) in enumerate(zip(spans, blocks)):
        held[pl.ds(plan[plan_at + i], n // TILE)] = b[lo : lo + n].reshape(n // TILE, TILE, TILE)

    def step(g, _):
        load(g).wait()
        products = []
        for u in range(GROUP):
            t = g * GROUP + u
            if transpose:
                products.append((plan[1 + slots + t], dot(held[plan[1 + t]], tiles[t])))
            else:
                products.append((plan[1 + t], dot(tiles[t], held[plan[1 + slots + t]])))
        for u, (target, product) in enumerate(products):
            target = jnp.where(g * GROUP + u < count, target, segments)
            total[target] += product
        return 0

    def unused(g, _):
        load(g).wait()
        return 0

    used = (count + GROUP - 1) // GROUP
    lax.fori_loop(0, used, step, 0)
    at = plan_at + len(spans)
    for out in outs:
        for k in range(0, out.shape[0], ROWS):
            block = total[pl.ds(plan[at], PER)].astype(BF16)
            out[pl.ds(k, ROWS)] = block.reshape(ROWS, TILE)
            at += 1
    lax.fori_loop(used, chunks, unused, 0)


def tile_sum(tiles, plan, plan_at, ins, outs, segments, transpose):
    slots = tiles.shape[2]
    vmem = pl.BlockSpec(memory_space=pltpu.VMEM)
    return pl.pallas_call(
        functools.partial(tiles_kernel, transpose, [i[1:] for i in ins], plan_at, segments),
        out_shape=[shape(n * ROWS, TILE) for n in outs],
        in_specs=[pl.BlockSpec(memory_space=pltpu.SMEM), pl.BlockSpec(memory_space=pltpu.HBM)]
        + [vmem] * len(ins),
        out_specs=[vmem] * len(outs),
        scratch_shapes=[
            pltpu.VMEM((slots, TILE, TILE), BF16),
            pltpu.VMEM((segments, TILE, TILE), BF16),
            pltpu.VMEM((segments + 1, TILE, TILE), F32),
            pltpu.SemaphoreType.DMA((slots // GROUP,)),
        ],
        compiler_params=pltpu.CompilerParams(vmem_limit_bytes=40 << 20),
        cost_estimate=pl.CostEstimate(
            flops=2 * slots * TILE**3, bytes_accessed=slots * TILE * TILE * 2, transcendentals=0
        ),
        name="tile_sum_t" if transpose else "tile_sum",
    )(plan, tiles, *[i[0] for i in ins])


def packed(weight, bias):
    high = bias.astype(BF16)
    low = (bias - high.astype(F32)).astype(BF16)
    rest = jnp.zeros((EXTRA - TILE - 2, TILE), BF16)
    return jnp.concatenate([weight.astype(BF16), high, low, rest], axis=0)


def unpacked(rows):
    rows = rows.astype(F32)
    return rows[:TILE], rows[TILE : TILE + 1] + rows[TILE + 1 : TILE + 2]


def total_of(offsets, parts):
    return summed([p[lo : lo + ROWS].astype(F32) for lo, p in zip(offsets, parts)])


def act_kernel(offsets, *refs):
    order_ref, cot_ref, weight_ref, bias_ref = refs[:4]
    parts = refs[4:-2]
    out_ref, act_ref = refs[-2:]
    nodes = cot_ref.shape[0]
    cot = dot(one_hot_t(order_ref, nodes), cot_ref[...], ((0,), (0,)))
    total = total_of(offsets, parts)
    hi = total.astype(BF16)
    lo = (total - hi.astype(F32)).astype(BF16)
    weight = weight_ref[...]
    pre = dot(hi, weight) + dot(lo, weight) + bias_ref[...]
    sig = jax.nn.sigmoid(pre)
    grad = cot * (sig * (1.0 + pre * (1.0 - sig)))
    act_ref[...] = (pre * sig).astype(BF16)
    weight_grad = jnp.zeros((TILE, TILE), F32)
    for t in range(0, nodes, TILE):
        grad_t = grad[t : t + TILE].T.astype(BF16)
        out_ref[t : t + TILE] = grad_t
        weight_grad += dot(grad_t, hi[t : t + TILE]) + dot(grad_t, lo[t : t + TILE])
    out_ref[nodes:] = packed(weight_grad, jnp.sum(grad, axis=0, keepdims=True))


def restore_kernel(order_ref, act_ref, out_ref):
    out_ref[...] = dot(one_hot_t(order_ref, act_ref.shape[0]), act_ref[...]).astype(BF16)


def input_kernel(offsets, *refs):
    order_ref, weight_ref = refs[:2]
    parts = refs[2:-1]
    out_ref = refs[-1]
    nodes = out_ref.shape[0]
    grad = total_of(offsets, parts).astype(BF16)
    back = jnp.concatenate(
        [dot(weight_ref[...], grad[t : t + TILE]).astype(BF16) for t in range(0, nodes, TILE)],
        axis=1,
    )
    out_ref[...] = dot(one_hot_t(order_ref, nodes), back, ((1,), (1,))).astype(BF16)


def add_kernel(spans, *refs):
    parts, out = refs[:-1], refs[-1]
    cuts = sorted({c for at, _, n in spans for c in (at, at + n)})
    for a, b in zip(cuts, cuts[1:]):
        terms = [
            p[lo + a - at : lo + b - at].astype(F32)
            for (at, lo, n), p in zip(spans, parts)
            if at <= a and b <= at + n
        ]
        out[a:b] = summed(terms).astype(out.dtype)


def added(rows, *parts):
    return call(
        functools.partial(add_kernel, [(at, lo, n) for at, _, lo, n in parts]),
        shape(rows, TILE),
        "add",
        *[p[1] for p in parts],
    )


def joined(*parts):
    if parts[0][0] is None:
        return None
    at, spans = 0, []
    for a, lo, n in parts:
        spans.append((at, a, lo, n))
        at += n
    return added(at, *spans)


def slab_kernel(offsets, plan_at, *refs):
    plan, parts, outs, held = refs[0], refs[1 : 1 + len(offsets)], refs[1 + len(offsets) : -1], refs[-1]
    for i, (lo, p) in enumerate(zip(offsets, parts)):
        held[plan[plan_at + i]] = p[lo : lo + EXTRA]
    pairs = [unpacked(held[i]) for i in range(len(offsets))]
    weight, bias = summed([p[0] for p in pairs]), summed([p[1] for p in pairs])
    if len(outs) == 1:
        outs[0][...] = packed(weight, bias)
    else:
        outs[0][...] = weight.T
        outs[1][...] = bias


def slab_sum(plan, plan_at, parts, out_shape):
    vmem = pl.BlockSpec(memory_space=pltpu.VMEM)
    return pl.pallas_call(
        functools.partial(slab_kernel, [p[1] for p in parts], plan_at),
        out_shape=out_shape,
        in_specs=[pl.BlockSpec(memory_space=pltpu.SMEM)] + [vmem] * len(parts),
        out_specs=[vmem] * len(out_shape),
        scratch_shapes=[pltpu.VMEM((len(parts), EXTRA, TILE), BF16)],
        compiler_params=pltpu.CompilerParams(vmem_limit_bytes=32 << 20),
        name="slab",
    )(plan, *[p[0] for p in parts])


def chip_kernel(a_ref, b_ref, out_ref):
    (weight_a, bias_a), (weight_b, bias_b) = unpacked(a_ref[...]), unpacked(b_ref[...])
    out_ref[...] = packed(weight_a + weight_b, bias_a + bias_b)


def call(kernel, out_shape, name, *args):
    vmem = pl.BlockSpec(memory_space=pltpu.VMEM)
    return pl.pallas_call(
        kernel,
        out_shape=out_shape,
        in_specs=[vmem] * len(args),
        out_specs=jax.tree.map(lambda _: vmem, out_shape),
        compiler_params=pltpu.CompilerParams(vmem_limit_bytes=32 << 20),
        name=name,
    )(*args)


def shape(*dims, dtype=BF16):
    return jax.ShapeDtypeStruct(dims, dtype)


def gather_row(mine, place, up, plan=None):
    n = ROWS
    near = {(0, 0): mine}
    for dy in (2, 1, -1):
        near[dy, 0] = shifted(mine, "y", dy)
    near[0, 1] = shifted(mine, "xh", 1)
    near[2, 1] = shifted(near[2, 0], "xh", 1)
    if plan is not None:
        near[0, 1] = after(near[0, 1], plan)
    for dy in (1, -1):
        near[dy, 1] = shifted(near[0, 1], "y", dy)
    out = []
    for (dy, dx), b in near.items():
        out.append((place(ROW, (-dy, -dx, 0)), b, 0, n))
        out.append((place(ROW, (-dy, -dx, 1)), twin(b), 0, n))
    return out


COL_ORDER = (4, 3, -3, 2, -2, 1, -1, 0)


def col_targets(place):
    return [[place(COL, (x, d))] for x in (0, 1) for d in COL_ORDER]


def scatter_col(pieces):
    n = ROWS
    o = dict(zip(COL_ORDER, pieces[:8]))
    t = dict(zip(COL_ORDER, pieces[8:]))
    r = {d: shifted(t[d], "xl", 1) for d in (4, 3, -3, 2, -2)}
    near = [shifted(t[d], "z", d) for d in (1, -1)]
    last = [shifted(o[d], "z", d) for d in (1, -1)]
    four = shifted(added(n, (0, o[4], 0, n), (0, r[4], 0, n)), "z", 4)
    threes = {
        2 * s: shifted(added(n, (0, o[3 * s], 0, n), (0, r[3 * s], 0, n)), "z", s)
        for s in (1, -1)
    }
    twos = [
        shifted(
            added(n, (0, o[d], 0, n), (0, r[d], 0, n), (0, threes[d], 0, n)), "z", d
        )
        for d in (2, -2)
    ]
    side = shifted(added(n, (0, t[0], 0, n), *[(0, a, 0, n) for a in near]), "xl", 1)
    return [(a, 0) for a in [o[0], side, four] + last + twos]


def gather_col(mine, place, hook=None):
    n = ROWS

    def block(x):
        return None if x is None else x[:n]

    z = {0: mine}
    for d in (2, -2):
        z[d] = shifted(mine, "z", d)
    x = {0: shifted(block(mine), "xl", 1)}
    if hook is not None:
        hook(x[0])
    for d in (4, 1, -1):
        z[d] = shifted(mine, "z", d)
    z[3] = shifted(z[2], "z", 1)
    z[-3] = shifted(z[-2], "z", -1)
    for d in (1, -1):
        x[d] = shifted(x[0], "z", d)
    for d in (2, -2, 4, 3, -3):
        x[d] = shifted(block(z[d]), "xl", 1)
    if hook is not None:
        hook([x[d] for d in (2, -2)])
    out = [(place(COL, (0, -d)), b, 0, n) for d, b in z.items()]
    out += [(place(COL, (1, -d)), b, 0, n) for d, b in x.items()]
    return out, [(place(("z",), (-d,)), b, n) for d, b in z.items()]


def row_targets(place):
    def at(c, *chips):
        return [place(ROW, chip + (c,)) for chip in chips]

    up, down = ((1, 1), (1, 0)), ((-1, 1), (-1, 0))
    rest = ((2, 1), (2, 0), (0, 1), (0, 0))
    return [
        at(1, rest[0]),
        at(1, *up, *down),
        at(1, *rest[1:]),
        at(0, *up),
        at(0, *down),
        at(0, *rest),
    ]


CHIPS = ((0, 0), (-1, 0), (1, 0), (0, 1), (2, 0), (2, 1), (-1, 1), (1, 1))


def scatter_row(pieces, sums):
    n, e = ROWS, EXTRA
    corner_t, near_t, rest_t, up, down, rest = pieces
    corner_t, near_t, rest_t = twin(corner_t), twin(near_t), twin(rest_t)
    corner = added(n + e, (0, rest, 0, n), (0, corner_t, 0, n), (n, sums, 0, e))
    corner = shifted(corner, "xh", 1)
    up = added(2 * n + e, (0, up, 0, 2 * n), (0, near_t, 0, 2 * n), (2 * n, sums, 0, e))
    up = shifted(up, "y", 1)
    down = added(2 * n + e, (0, down, 0, 2 * n), (0, near_t, 2 * n, 2 * n), (2 * n, sums, 0, e))
    down = shifted(down, "y", -1)
    far = added(
        n + 2 * e,
        (0, rest, n, n),
        (0, rest_t, 0, n),
        (0, corner, 0, n),
        (n, sums, 0, e),
        (n + e, corner, n, e),
    )
    far = shifted(far, "y", 2)
    side = added(
        n + 2 * e,
        (0, rest, 2 * n, n),
        (0, rest_t, n, n),
        (0, up, 0, n),
        (0, down, 0, n),
        (n, up, 2 * n, e),
        (n + e, down, 2 * n, e),
    )
    side = shifted(side, "xh", 1)
    parts = [(rest, 3 * n), (rest_t, 2 * n), (up, n), (down, n), (far, 0), (side, 0)]
    extra = [(sums, 0), (up, 2 * n), (down, 2 * n), (corner, n)]
    return parts, extra + [(a, at) for a in (far, side) for at in (n, n + e)]


def on_device(
    features, node_order, weight, bias, tile_values, tile_rows, tile_cols, tile_count, cotangent
):
    nodes, width = features.shape
    order = node_order.reshape(1, nodes)
    me = {a: lax.axis_index(a) for a in ALL}
    up = 1 - 2 * me["core"]

    def place(axes, delta):
        at = 0
        for a, d in zip(axes, delta):
            at = at * SIZES[a] + lax.rem(me[a] + d + SIZES[a], SIZES[a])
        return at * PER

    slab_tiles = SIZES["xl"] * SIZES["z"] * PER
    col_blocks, col_extra = gather_col(None, place)
    sections = [
        [h[0] for h in gather_row(None, place, up)] + [at for out in col_targets(place) for at in out],
        [h[0] for h in col_blocks] + [at for out in row_targets(place) for at in out],
        [h[0] // PER for h in col_extra],
        [place(("y", "xh"), d) // PER for d in CHIPS],
    ]
    numbers = [tile_count.reshape(1), tile_rows.reshape(-1), tile_cols.reshape(-1)]
    plan_at = [1 + 2 * tile_values.shape[2]]
    for here in sections:
        numbers.append(jnp.stack(here).astype(jnp.int32))
        plan_at.append(plan_at[-1] + len(here))
    plan = jnp.concatenate(numbers)

    ordered = features.at[order[0]].get(mode="promise_in_bounds")
    pieces = tile_sum(
        tile_values,
        plan,
        plan_at[0],
        [h[1:] for h in gather_row(ordered, place, up, plan)],
        [len(o) for o in col_targets(place)],
        slab_tiles,
        False,
    )
    parts = scatter_col(pieces)
    block, act = call(
        functools.partial(act_kernel, [p[1] for p in parts]),
        [shape(nodes + EXTRA, width), shape(nodes, width)],
        "act",
        order,
        cotangent,
        weight,
        bias.reshape(1, width),
        *[p[0] for p in parts],
    )
    tokens = []
    blocks, extra = gather_col(block, place, tokens.append)
    activated = call(
        restore_kernel, shape(nodes, width), "restore", order, act
    )
    gathered = [e[1:] for e in extra]
    gathered[0] = (after(gathered[0][0], *tokens[1]), gathered[0][1])
    (sums,) = slab_sum(plan, plan_at[2], gathered, [shape(EXTRA, width)])
    pair = call(chip_kernel, shape(EXTRA, width), "pair", sums, shifted(sums, "xl", 1))
    pieces = tile_sum(
        tile_values,
        after(plan, sums),
        plan_at[1],
        [b[1:] for b in blocks],
        [len(o) for o in row_targets(place)],
        slab_tiles,
        True,
    )
    sums = call(chip_kernel, shape(EXTRA, width), "chip", pair, twin(pair))
    parts, extra = scatter_row(pieces, sums)
    input_grad = call(
        functools.partial(input_kernel, [p[1] for p in parts]),
        shape(nodes, width),
        "input",
        order,
        weight,
        *[p[0] for p in parts],
    )
    weight_grad, bias_grad = slab_sum(
        plan,
        plan_at[3],
        extra,
        [shape(width, width, dtype=F32), shape(1, width, dtype=F32)],
    )
    return activated, input_grad, weight_grad, bias_grad.reshape(width)


def solution(mesh):
    fine = Mesh(mesh.devices.reshape([SIZES[a] for a in ALL]), ALL)
    in_specs = (
        P(ALL, None),
        P(ROW, COL, None),
        P(),
        P(),
        P(ROW, COL, None, None, None),
        P(ROW, COL, None),
        P(ROW, COL, None),
        P(ROW, COL),
        P(ALL, None),
    )
    out_specs = (P(ALL, None), P(ALL, None), P(), P())
    return jax.shard_map(
        on_device, mesh=fine, in_specs=in_specs, out_specs=out_specs, check_vma=False
    )
```
